32 devices in a mesh: groups: 2 (over x), slab: 8 (over z, y), ray: 2 (over core).
Axes of the slice: x: 2, y: 2, z: 4, core: 2. Of those that a mesh axis runs over, the one named last changes fastest.
Arguments:
- features: bfloat16 [8, 64, 8, 4096], P('slab', None, None, ('groups', 'ray')), parts along dimension 3, may hold values from -6 to 6
- spacing: float32 [8, 8, 4096], P('slab', None, ('groups', 'ray')), parts along dimension 2, may hold values from 0.004 to 0.04
- live_counts: int32 [8, 4096], P('slab', ('groups', 'ray')), parts along dimension 1, may hold values from 0 to 8
- direction: int32 [4096], P(('groups', 'ray')), parts along dimension 0, may hold values from 0 to 1
- cotangent: float32 [96, 4096], P(None, ('groups', 'ray')), parts along dimension 1, may hold values from -20 to 20
- first_weight: bfloat16 [8, 256, 64], P('slab'), may hold values from -0.75 to 0.75
- first_bias: float32 [8, 256], P('slab'), may hold values from -3 to 3
- second_weight: bfloat16 [8, 256, 256], P('slab'), may hold values from -0.375 to 0.375
- second_bias: float32 [8, 256], P('slab'), may hold values from -3 to 3
- color_weight: bfloat16 [8, 96, 256], P('slab'), may hold values from -0.375 to 0.375
- color_bias: float32 [8, 96], P('slab'), may hold values from -4 to 4
- sigma_weight: bfloat16 [8, 256], P('slab'), may hold values from -0.375 to 0.375
- sigma_bias: float32 [8], P('slab'), may hold values from -1 to 1
Outputs:
- feature_grad: bfloat16 [8, 64, 8, 4096], P('slab', None, None, ('groups', 'ray')), parts along dimension 3
- density_grad: float32 [8, 8, 4096], P('slab', None, ('groups', 'ray')), parts along dimension 2
- radiance_grad: bfloat16 [8, 96, 8, 4096], P('slab', None, None, ('groups', 'ray')), parts along dimension 3
- first_grad: float32 [16, 256, 64], P(('groups', 'slab'), 'ray'), parts along dimension 0
- second_grad: float32 [16, 256, 256], P(('groups', 'slab'), 'ray'), parts along dimension 0
- color_grad: float32 [16, 256, 96], P(('groups', 'slab'), 'ray'), parts along dimension 0
- sigma_grad: float32 [16, 256], P(('groups', 'slab'), 'ray'), parts along dimension 0
The draws below stay inside these ranges and needn't reach their ends.
There are 2 independent parts, one for each index of `groups`. The reference program is written for one: setup_inputs(seed, part) draws one part's arguments, and reference() takes and returns one part's arrays. A program takes and returns all parts, laid end to end along the dimension named above; an argument that names none is the same for every part. Nothing has to cross between parts.
Inputs may be any that keep to these rules, and one draw needn't show every extreme that they name: The first live_counts slots of a ray in a slab hold its samples. `direction`: 0: the ray meets the slabs in rising index order; 1: in falling order.
All inputs are finite; a program needn't handle non-finite values.
Results may differ from the reference program's by a relative error of at most 0.0067.
Values sent between devices are 32-bit elements; how exact they have to be, the bound alone decides.
A program may use at most 128 MiB of HBM per device.

```python
import math
import jax
import jax.numpy as jnp
from jax import lax

FEAT = 64
HID = 256
CH = 96
K = 8
RAYS = 2048
SLABS = 8


def with_ends(entries, rng, low, high):
    shape = entries.shape
    spot = [jax.random.randint(jax.random.fold_in(rng, axis), (), 0, shape[axis]) for axis in range(len(shape))]
    entries = entries.at[tuple(spot)].set(low)
    longest = shape.index(max(shape))
    spot[longest] = (spot[longest] + 1) % shape[longest]
    return entries.at[tuple(spot)].set(high)


def levels(key, dims, split, least, high):
    factor_of = 1.0
    for dim, parts in split:
        draws = jax.random.uniform(jax.random.fold_in(jax.random.fold_in(key, 6), dim), (parts,), jnp.float32, least / len(split), high / len(split))
        factor_of = factor_of * jnp.repeat(jnp.exp(draws), dims[dim] // parts).reshape((-1,) + (1,) * (len(dims) - 1 - dim))
    return factor_of


def gaussian(rng, dims, scale, bound, pieces=(), kind=jnp.bfloat16):
    gain = levels(rng, dims, pieces, -0.22, 0.18) if pieces else 1.0
    values = jax.random.normal(rng, dims, jnp.float32) * scale * gain
    return jnp.minimum(jnp.maximum(values, -bound), bound).astype(kind)


def setup_inputs(seed: int = 0, part: int = 0) -> dict:
    streams_of = jax.random.split(jax.random.key(seed), 14)
    part_keys = jax.random.split(jax.random.fold_in(streams_of[13], part), 14)
    features = gaussian(part_keys[0], (SLABS, FEAT, K, RAYS), 1.0, 6.0, ((0, 8), (3, 2)))
    spacing = jnp.clip(jnp.exp(math.log(0.04) - 2.30258502 * jax.random.uniform(part_keys[1], (SLABS, K, RAYS), jnp.float32) ** levels(part_keys[1], (SLABS, K, RAYS), ((0, 8), (2, 2)), -0.2, 0.2)), 0.004, 0.04)
    live_counts = with_ends(jax.random.randint(part_keys[2], (SLABS, RAYS), 0, K + 1), jax.random.fold_in(part_keys[2], 1), 0, K).astype(jnp.int32)
    direction = with_ends(jax.random.randint(part_keys[3], (RAYS,), 0, 2), jax.random.fold_in(part_keys[3], 1), 0, 1).astype(jnp.int32)
    cotangent = jnp.clip(jax.random.uniform(part_keys[4], (CH, RAYS), jnp.float32, -20.0, 20.0) * levels(part_keys[4], (CH, RAYS), ((1, 2),), -0.4, 0.0), -20.0, 20.0)
    first_weight = gaussian(streams_of[5], (SLABS, HID, FEAT), FEAT ** -0.5, 0.75, ((0, 8),))
    first_bias = gaussian(streams_of[6], (SLABS, HID), 0.5, 3.0, ((0, 8),), jnp.float32)
    second_weight = gaussian(streams_of[7], (SLABS, HID, HID), HID ** -0.5, 0.375, ((0, 8),))
    second_bias = gaussian(streams_of[8], (SLABS, HID), 0.5, 3.0, ((0, 8),), jnp.float32)
    color_weight = gaussian(streams_of[9], (SLABS, CH, HID), HID ** -0.5, 0.375, ((0, 8),))
    color_bias = gaussian(streams_of[10], (SLABS, CH), 1.0, 4.0, ((0, 8),), jnp.float32)
    sigma_weight = gaussian(streams_of[11], (SLABS, HID), HID ** -0.5, 0.375, ((0, 8),))
    sigma_bias = jnp.clip(jax.random.uniform(streams_of[12], (SLABS,), jnp.float32, -1.0, 1.0) * levels(streams_of[12], (SLABS,), ((0, 8),), -0.4, 0.0), -1.0, 1.0)
    return {"features": features, "spacing": spacing, "live_counts": live_counts, "direction": direction, "cotangent": cotangent, "first_weight": first_weight, "first_bias": first_bias, "second_weight": second_weight, "second_bias": second_bias, "color_weight": color_weight, "color_bias": color_bias, "sigma_weight": sigma_weight, "sigma_bias": sigma_bias}


def silu_slope(values):
    gate = jax.nn.sigmoid(values)
    return gate * (1.0 + values * (1.0 - gate))


def hidden_layers(inputs, weight_a, bias_a, weight_b, bias_b):
    first_pre = jnp.dot(weight_a, inputs, preferred_element_type=jnp.float32) + bias_a[:, None]
    first_act = jax.nn.silu(first_pre).astype(jnp.bfloat16)
    second_pre = jnp.dot(weight_b, first_act, preferred_element_type=jnp.float32) + bias_b[:, None]
    second_act = jax.nn.silu(second_pre).astype(jnp.bfloat16)
    return first_pre, first_act, second_pre, second_act


def carry_step(carry, slab_items):
    slab_tau, slab_light = slab_items
    return slab_light + jnp.exp(-slab_tau)[None, :] * carry, carry


def reference(features, spacing, live_counts, direction, cotangent, first_weight, first_bias, second_weight, second_bias, color_weight, color_bias, sigma_weight, sigma_bias):
    def forward_slab(slab_items):
        inputs, weight_a, bias_a, weight_b, bias_b, weight_c, bias_c, weight_d, bias_d = slab_items
        flat_inputs = inputs.reshape(FEAT, K * RAYS)
        _, _, _, second_act = hidden_layers(flat_inputs, weight_a, bias_a, weight_b, bias_b)
        logits = jnp.dot(weight_c, second_act, preferred_element_type=jnp.float32) + bias_c[:, None]
        raw_part = jnp.dot(weight_d, second_act, preferred_element_type=jnp.float32) + bias_d
        return jax.nn.sigmoid(logits).reshape(CH, K, RAYS), raw_part.reshape(K, RAYS)

    radiance, raw_density = lax.map(forward_slab, (features, first_weight, first_bias, second_weight, second_bias, color_weight, color_bias, sigma_weight, sigma_bias))
    live = (jnp.arange(K, dtype=jnp.int32)[None, :, None] < live_counts[:, None, :]).astype(jnp.float32)
    depth = jax.nn.softplus(raw_density) * spacing * live
    inside = jnp.cumsum(depth, axis=1) - depth
    slab_depth = jnp.sum(depth, axis=1)
    opacity = 1.0 - jnp.exp(-depth)
    local = jnp.sum((jnp.exp(-inside) * opacity)[:, None] * radiance, axis=2)
    ascend = direction == 0
    lower = jnp.cumsum(slab_depth, axis=0) - slab_depth
    upper = jnp.sum(slab_depth, axis=0)[None] - lower - slab_depth
    prefix = jnp.where(ascend[None], lower, upper)
    empty = jnp.zeros((CH, RAYS), jnp.float32)
    _, after_rising = lax.scan(carry_step, empty, (slab_depth, local), reverse=True)
    _, after_falling = lax.scan(carry_step, empty, (slab_depth, local))
    suffix = jnp.where(ascend[None, None], after_rising, after_falling)
    transmit = jnp.exp(-(prefix[:, None] + inside))
    sample_weight = transmit * opacity
    radiance_full = sample_weight[:, None] * cotangent[None, :, None, :]
    radiance_grad = radiance_full.astype(jnp.bfloat16)
    projected = jnp.sum(cotangent[None, :, None, :] * radiance, axis=1)
    carried = sample_weight * projected
    behind_in = jnp.sum(carried, axis=1, keepdims=True) - jnp.cumsum(carried, axis=1)
    behind_out = jnp.exp(-(prefix + slab_depth)) * jnp.sum(cotangent[None] * suffix, axis=1)
    density_grad = (transmit * jnp.exp(-depth) * projected - behind_in - behind_out[:, None]) * spacing * live
    logit_grad = (radiance_full * radiance * (1.0 - radiance)).astype(jnp.bfloat16)
    raw_grad = (density_grad * jax.nn.sigmoid(raw_density)).astype(jnp.bfloat16)

    def backward_slab(slab_items):
        inputs, weight_a, bias_a, weight_b, bias_b, weight_c, weight_d, logit_part, raw_part = slab_items
        flat_inputs = inputs.reshape(FEAT, K * RAYS)
        first_pre, first_act, second_pre, second_act = hidden_layers(flat_inputs, weight_a, bias_a, weight_b, bias_b)
        logit_flat = logit_part.reshape(CH, K * RAYS)
        raw_flat = raw_part.reshape(K * RAYS)
        hidden_two = jnp.dot(weight_c.T, logit_flat, preferred_element_type=jnp.float32)
        hidden_two = hidden_two + weight_d[:, None].astype(jnp.float32) * raw_flat[None, :].astype(jnp.float32)
        second_delta = (hidden_two * silu_slope(second_pre)).astype(jnp.bfloat16)
        hidden_one = jnp.dot(weight_b.T, second_delta, preferred_element_type=jnp.float32)
        first_delta = (hidden_one * silu_slope(first_pre)).astype(jnp.bfloat16)
        feature_part = jnp.dot(weight_a.T, first_delta, preferred_element_type=jnp.float32).astype(jnp.bfloat16)
        first_part = jnp.dot(first_delta, flat_inputs.T, preferred_element_type=jnp.float32)
        second_part = jnp.dot(second_delta, first_act.T, preferred_element_type=jnp.float32)
        color_part = jnp.dot(second_act, logit_flat.T, preferred_element_type=jnp.float32)
        sigma_part = jnp.dot(second_act, raw_flat, preferred_element_type=jnp.float32)
        return feature_part.reshape(FEAT, K, RAYS), first_part, second_part, color_part, sigma_part

    feature_grad, first_grad, second_grad, color_grad, sigma_grad = lax.map(backward_slab, (features, first_weight, first_bias, second_weight, second_bias, color_weight, sigma_weight, logit_grad, raw_grad))
    return (feature_grad, density_grad, radiance_grad, first_grad, second_grad, color_grad, sigma_grad)
```

```python
import functools

import jax
import jax.numpy as jnp
from jax import lax
from jax.experimental import pallas as pl
from jax.experimental.pallas import tpu as pltpu
from jax.sharding import PartitionSpec as P

MESH = pl.DeviceIdType.MESH
F32 = jnp.float32
BF16 = jnp.bfloat16


def dot(a, b):
    return jnp.dot(a, b, preferred_element_type=F32)


def dot_nt(a, b):
    return lax.dot_general(a, b, (((1,), (1,)), ((), ())), preferred_element_type=F32)


def main_kernel(
    slabs, chunks, unroll,
    x_ref, gap_ref, live_ref, dir_ref, cot_ref, w1_ref, b1_ref, w2_ref, b2_ref,
    wc_ref, bc_ref, wd_ref, bd_ref,
    feat_ref, dens_ref, sw_ref, g1_ref, g2_ref, gc_ref, gs_ref,
    xp, fp, perm, w1h, w1t, w2h, w2t, wch, wct,
    a1, s1, a2, s2, mix, raw_s, proj_s, ins_s, beh_s, rg_s, sww,
    gath, gsum, grecv, send_sem, recv_sem, wsem,
):
    slots = gap_ref.shape[0]
    rays = gap_ref.shape[1]
    feat = w1_ref.shape[1]
    hid = w1_ref.shape[0]
    ch = wc_ref.shape[0]
    rb = rays // chunks
    half = hid // 2
    me = lax.axis_index("slab")
    ray = lax.axis_index("ray")
    other = 1 - ray

    barrier = pltpu.get_barrier_semaphore()

    def greet(step, carry):
        pl.semaphore_signal(
            barrier, inc=1, device_id={"slab": lax.rem(me + step, slabs)}, device_id_type=MESH
        )
        return carry

    lax.fori_loop(1, slabs, greet, 0)
    pl.semaphore_signal(barrier, inc=1, device_id={"ray": other}, device_id_type=MESH)

    w1h[...] = w1_ref[...] * 0.5
    w2h[...] = w2_ref[...] * 0.5
    w1t[...] = w1_ref[...].astype(F32).T.astype(BF16)
    w2t[...] = (w2_ref[...].astype(F32) * 0.5).T.astype(BF16)
    pad = wch.shape[0] - ch
    wrow = jnp.where(
        lax.broadcasted_iota(jnp.int32, (pad, hid), 0) == 0, wd_ref[...].astype(F32) * 0.5, 0.0
    )
    wch[0:ch, :] = wc_ref[...] * 0.5
    wch[ch:, :] = wrow.astype(BF16)
    wct[...] = wch[...].astype(F32).T.astype(BF16)
    b1h = b1_ref[...] * 0.5
    b2h = b2_ref[...] * 0.5
    bch = bc_ref[...] * 0.5

    rows = slots * feat
    to = lax.broadcasted_iota(jnp.int32, (rows, rows), 0)
    at = lax.broadcasted_iota(jnp.int32, (rows, rows), 1)
    perm[...] = jnp.where(at == lax.rem(to, feat) * slots + to // feat, 1.0, 0.0).astype(BF16)

    gsum[...] = jnp.zeros_like(gsum)

    def forward(c):
        span = pl.ds(c * rb, rb)
        xp[c] = dot(perm[...], x_ref[:, span]).astype(BF16)
        cot = cot_ref[:, span]
        cot_q = cot * 0.25
        cot_sum = jnp.sum(cot, axis=0, keepdims=True)

        def step(k, carry):
            xk = xp[c, pl.ds(pl.multiple_of(k * feat, feat), feat), :]
            u = dot(w1h[...], xk) + b1h
            t = jnp.tanh(u)
            p = 1.0 + t
            a = u * p
            a1[c, k] = a.astype(BF16)
            s1[c, k] = (p + a * (1.0 - t)).astype(BF16)
            u = dot(w2h[...], a1[c, k]) + b2h
            t = jnp.tanh(u)
            p = 1.0 + t
            a = u * p
            a2[c, k] = a.astype(BF16)
            s2[c, k] = (p + a * (1.0 - t)).astype(BF16)
            l = dot(wch[...], a2[c, k])
            t = jnp.tanh(l[0:ch] + bch)
            mix[c, k] = cot_q - cot_q * t * t
            raw_s[c, pl.ds(k, 1), :] = l[ch : ch + 1] * 2.0 + bd_ref[...]
            proj_s[c, pl.ds(k, 1), :] = 0.5 * (
                cot_sum + jnp.sum(cot * t, axis=0, keepdims=True)
            )
            return carry

        lax.fori_loop(0, slots, step, 0, unroll=unroll)

    def depth_of(c):
        span = pl.ds(c * rb, rb)
        raw = raw_s[c]
        live = (
            lax.broadcasted_iota(jnp.int32, raw.shape, 0) < live_ref[:, span]
        ).astype(F32)
        scale = gap_ref[:, span] * live
        soft = jnp.maximum(raw, 0.0) + jnp.log1p(jnp.exp(-jnp.abs(raw)))
        return raw, scale, soft * scale

    def summarize(c):
        raw, scale, depth = depth_of(c)
        total = jnp.zeros((1, rb), F32)
        for k in range(slots):
            ins_s[c, k : k + 1, :] = total
            total = total + depth[k : k + 1]
        weight = jnp.exp(-ins_s[c]) * (1.0 - jnp.exp(-depth))
        gath[c, me, 0:1, :] = total
        gath[c, me, 1:2, :] = jnp.sum(weight * proj_s[c], axis=0, keepdims=True)

    def copy_to(c, step):
        return pltpu.make_async_remote_copy(
            src_ref=gath.at[c, me],
            dst_ref=gath.at[c, me],
            send_sem=send_sem.at[c, step],
            recv_sem=recv_sem.at[c, step],
            device_id={"slab": lax.rem(me + step, slabs)},
            device_id_type=MESH,
        )

    def send(c):
        def go(step, carry):
            copy_to(c, step).start()
            return carry

        lax.fori_loop(1, slabs, go, 0)

    def receive(c):
        def go(step, carry):
            copy_to(c, step).wait()
            return carry

        lax.fori_loop(1, slabs, go, 0)

    def settle(c):
        span = pl.ds(c * rb, rb)
        raw, scale, depth = depth_of(c)
        zero = jnp.zeros((1, rb), F32)
        before, after, up, down = zero, zero, zero, zero
        for s in range(slabs):
            tau = gath[c, s, 0:1, :]
            light = gath[c, s, 1:2, :]
            before = before + jnp.where(s < me, tau, 0.0)
            after = after + jnp.where(s > me, tau, 0.0)
            down = jnp.where(s < me, light + jnp.exp(-tau) * down, down)
        for s in reversed(range(slabs)):
            tau = gath[c, s, 0:1, :]
            light = gath[c, s, 1:2, :]
            up = jnp.where(s > me, light + jnp.exp(-tau) * up, up)
        ascend = dir_ref[:, span] == 0
        prefix = jnp.where(ascend, before, after)
        behind = jnp.where(ascend, up, down)
        behind_out = jnp.exp(-(prefix + gath[c, me, 0:1, :])) * behind
        transmit = jnp.exp(-(prefix + ins_s[c]))
        fade = jnp.exp(-depth)
        weight = transmit * (1.0 - fade)
        sww[c] = weight
        sw_ref[:, span] = weight
        proj = proj_s[c]
        carried = weight * proj
        total = behind_out
        for k in reversed(range(slots)):
            beh_s[c, k : k + 1, :] = total
            total = total + carried[k : k + 1]
        dens = (transmit * fade * proj - beh_s[c]) * scale
        dens_ref[:, span] = dens
        rg_s[c] = dens * (0.5 * jnp.tanh(0.5 * raw) + 0.5)

    def backward(c):
        first_row = lax.broadcasted_iota(jnp.int32, (pad, rb), 0) == 0

        def step(k, carry):
            lg = mix[c, k] * sww[c, pl.ds(k, 1), :]
            tail = jnp.where(first_row, rg_s[c, pl.ds(k, 1), :], 0.0)
            lga = jnp.concatenate([lg.astype(BF16), tail.astype(BF16)], axis=0)
            d2 = (dot(wct[...], lga) * s2[c, k].astype(F32)).astype(BF16)
            d1 = (dot(w2t[...], d2) * s1[c, k].astype(F32)).astype(BF16)
            at_k = pl.ds(pl.multiple_of(k * feat, feat), feat)
            fp[c, at_k, :] = dot(w1t[...], d1).astype(BF16)
            gsum[:, 0:hid] += dot_nt(d2, a1[c, k])
            gsum[:, hid : hid + ch + pad] += dot_nt(a2[c, k], lga)
            gsum[:, hid + ch + pad : hid + ch + pad + feat] += dot_nt(d1, xp[c, at_k, :])
            return carry

        lax.fori_loop(0, slots, step, 0, unroll=unroll)

    for c in range(chunks):
        forward(c)
        summarize(c)
        if c == 0:
            pl.semaphore_wait(barrier, slabs)
        send(c)
    for c in range(chunks):
        receive(c)
        settle(c)
        backward(c)

    give = pltpu.make_async_remote_copy(
        src_ref=gsum.at[pl.ds(pl.multiple_of(other * half, half), half)],
        dst_ref=grecv,
        send_sem=wsem.at[0],
        recv_sem=wsem.at[1],
        device_id={"ray": other},
        device_id_type=MESH,
    )
    give.start()
    for c in range(chunks):
        feat_ref[:, pl.ds(c * rb, rb)] = lax.dot_general(
            perm[...], fp[c], (((0,), (0,)), ((), ())), preferred_element_type=F32
        ).astype(BF16)
    give.wait()
    both = gsum[pl.ds(pl.multiple_of(ray * half, half), half), :] + grecv[...]
    g2_ref[...] = both[:, 0:hid]
    gc_ref[...] = both[:, hid : hid + ch]
    g1_ref[...] = both[:, hid + ch + pad : hid + ch + pad + feat]
    same = lax.broadcasted_iota(jnp.int32, (half, half), 0) == lax.broadcasted_iota(
        jnp.int32, (half, half), 1
    )
    gs_ref[...] = jnp.sum(
        jnp.where(same, both[:, hid + ch : hid + ch + 1], 0.0), axis=0, keepdims=True
    )


def body(
    slabs, features, spacing, live_counts, direction, cotangent, first_weight, first_bias,
    second_weight, second_bias, color_weight, color_bias, sigma_weight, sigma_bias,
):
    _, feat, slots, rays = features.shape
    hid = first_weight.shape[1]
    ch = color_weight.shape[1]
    padded = 128
    chunks = 2
    rb = rays // chunks
    half = hid // 2
    wide = hid + padded + 128
    rows = slots * feat
    vm = pl.BlockSpec(memory_space=pltpu.VMEM)
    S = jax.ShapeDtypeStruct
    V = pltpu.VMEM
    outs = pl.pallas_call(
        functools.partial(main_kernel, slabs, chunks, 2),
        out_shape=(
            S((rows, rays), BF16), S((slots, rays), F32), S((slots, rays), F32),
            S((half, feat), F32), S((half, hid), F32), S((half, ch), F32), S((1, half), F32),
        ),
        in_specs=[vm] * 13,
        out_specs=(vm,) * 7,
        scratch_shapes=[
            V((chunks, rows, rb), BF16), V((chunks, rows, rb), BF16), V((rows, rows), BF16),
            V((hid, feat), BF16), V((feat, hid), BF16), V((hid, hid), BF16), V((hid, hid), BF16),
            V((padded, hid), BF16), V((hid, padded), BF16),
            V((chunks, slots, hid, rb), BF16), V((chunks, slots, hid, rb), BF16),
            V((chunks, slots, hid, rb), BF16), V((chunks, slots, hid, rb), BF16),
            V((chunks, slots, ch, rb), F32),
            V((chunks, slots, rb), F32), V((chunks, slots, rb), F32), V((chunks, slots, rb), F32),
            V((chunks, slots, rb), F32), V((chunks, slots, rb), F32), V((chunks, slots, rb), F32),
            V((chunks, slabs, 2, rb), F32),
            V((hid, wide), F32), V((half, wide), F32),
            pltpu.SemaphoreType.DMA((chunks, slabs)),
            pltpu.SemaphoreType.DMA((chunks, slabs)),
            pltpu.SemaphoreType.DMA((2,)),
        ],
        compiler_params=pltpu.CompilerParams(
            collective_id=0, has_side_effects=True, vmem_limit_bytes=48 * 1024 * 1024
        ),
    )(
        features.reshape(rows, rays), spacing[0], live_counts, direction[None], cotangent,
        first_weight[0], first_bias.reshape(hid, 1), second_weight[0],
        second_bias.reshape(hid, 1), color_weight[0], color_bias.reshape(ch, 1),
        sigma_weight, sigma_bias.reshape(1, 1),
    )
    feature_grad, dens, weight, g1, g2, gc, gs = outs
    radiance_grad = (weight[None] * cotangent[:, None, :]).astype(BF16)
    return (
        feature_grad.reshape(1, feat, slots, rays), dens[None], radiance_grad[None],
        g1[None], g2[None], gc[None], gs,
    )


def solution(mesh):
    rays = P(("groups", "ray"))
    in_specs = (
        P("slab", None, None, ("groups", "ray")),
        P("slab", None, ("groups", "ray")),
        P("slab", ("groups", "ray")),
        rays,
        P(None, ("groups", "ray")),
        P("slab", None, None),
        P("slab", None),
        P("slab", None, None),
        P("slab", None),
        P("slab", None, None),
        P("slab", None),
        P("slab", None),
        P("slab"),
    )
    out_specs = (
        P("slab", None, None, ("groups", "ray")),
        P("slab", None, ("groups", "ray")),
        P("slab", None, None, ("groups", "ray")),
        P(("groups", "slab"), "ray", None),
        P(("groups", "slab"), "ray", None),
        P(("groups", "slab"), "ray", None),
        P(("groups", "slab"), "ray"),
    )
    return jax.shard_map(
        functools.partial(body, mesh.shape["slab"]),
        mesh=mesh,
        in_specs=in_specs,
        out_specs=out_specs,
        check_vma=False,
    )
```

```python
import functools

import jax
import jax.numpy as jnp
from jax import lax
from jax.experimental import pallas as pl
from jax.experimental.pallas import tpu as pltpu
from jax.sharding import PartitionSpec as P

MESH = pl.DeviceIdType.MESH
F32 = jnp.float32
BF16 = jnp.bfloat16
CHUNKS = 2
UNROLL = 8


def dot(a, b):
    return jnp.dot(a, b, preferred_element_type=F32)


def dot_nt(a, b):
    return lax.dot_general(a, b, (((1,), (1,)), ((), ())), preferred_element_type=F32)


def main_kernel(
    slabs, chunks, unroll,
    bd_ref, x_hbm, gap_hbm, live_hbm, dir_hbm, cot_hbm, w1_hbm, b1_hbm, w2_hbm, b2_hbm,
    wc_hbm, bc_hbm, wd_hbm,
    feat_ref, dens_ref, sw_ref, g1_ref, g2_ref, gc_ref, gs_ref,
    x_ref, gap_ref, live_ref, dir_ref, cot_ref, w1_ref, b1_ref, w2_ref, b2_ref,
    wc_ref, bc_ref, wd_ref, in_sem,
    xp, fp, perm, permt, w1h, w1t, w2h, w2t, wch, wct,
    a1, s1, a2, s2, d1_s, d2_s, mix, raw_s, proj_s, ins_s, beh_s, rg_s, sww,
    gath, gsum, grecv, send_sem, recv_sem, wsem,
):
    slots = gap_ref.shape[0]
    rays = gap_ref.shape[1]
    feat = w1_ref.shape[0]
    hid = w1_ref.shape[1]
    ch = wc_ref.shape[0]
    rb = rays // chunks
    half = hid // 2
    me = lax.axis_index("slab")
    ray = lax.axis_index("ray")
    other = 1 - ray

    loads = [
        pltpu.make_async_copy(src, dst, in_sem.at[i])
        for i, (src, dst) in enumerate(
            (
                (x_hbm, x_ref), (w1_hbm, w1_ref), (b1_hbm, b1_ref), (w2_hbm, w2_ref),
                (b2_hbm, b2_ref), (wc_hbm, wc_ref), (bc_hbm, bc_ref), (wd_hbm, wd_ref),
                (cot_hbm, cot_ref), (gap_hbm, gap_ref), (live_hbm, live_ref), (dir_hbm, dir_ref),
            )
        )
    ]
    for load in loads:
        load.start()

    barrier = pltpu.get_barrier_semaphore()

    def greet(step, carry):
        pl.semaphore_signal(
            barrier, inc=1, device_id={"slab": lax.rem(me + step, slabs)}, device_id_type=MESH
        )
        return carry

    lax.fori_loop(1, slabs, greet, 0)
    pl.semaphore_signal(barrier, inc=1, device_id={"ray": other}, device_id_type=MESH)

    first = lax.broadcasted_iota(jnp.int32, (feat, slots * feat), 0) * slots
    at = lax.broadcasted_iota(jnp.int32, (feat, slots * feat), 1)
    for k in range(slots):
        perm[k * feat : (k + 1) * feat, :] = jnp.where(at == first + k, 1.0, 0.0).astype(BF16)
    for load in loads[1:]:
        load.wait()

    w1h[...] = (w1_ref[...].astype(F32) * 0.5).T.astype(BF16)
    w2h[...] = w2_ref[...] * 0.5
    pad = wch.shape[0] - ch
    wrow = jnp.where(
        lax.broadcasted_iota(jnp.int32, (pad, hid), 0) == 0, wd_ref[...].astype(F32) * 0.5, 0.0
    )
    wch[0:ch, :] = wc_ref[...] * 0.5
    wch[ch:, :] = wrow.astype(BF16)

    def column(row):
        n = row.shape[1]
        return jnp.broadcast_to(row * 0.5, (8, n)).T[:, 0:1]

    b1h = column(b1_ref[...])
    b2h = column(b2_ref[...])
    bch = column(bc_ref[...])
    loads[0].wait()

    def forward(c):
        span = pl.ds(c * rb, rb)
        xp[c] = dot(perm[...], x_ref[:, span]).astype(BF16)
        cot = cot_ref[:, span]
        cot_q = cot * 0.25
        cot_sum = jnp.sum(cot, axis=0, keepdims=True)

        def step(k, carry):
            xk = xp[c, pl.ds(pl.multiple_of(k * feat, feat), feat), :]
            u = dot(w1h[...], xk) + b1h
            t = jnp.tanh(u)
            p = 1.0 + t
            a = u * p
            a1[c, k] = a.astype(BF16)
            s1[c, k] = (p + a * (1.0 - t)).astype(BF16)
            u = dot(w2h[...], a1[c, k]) + b2h
            t = jnp.tanh(u)
            p = 1.0 + t
            a = u * p
            a2[c, k] = a.astype(BF16)
            s2[c, k] = (p + a * (1.0 - t)).astype(BF16)
            l = dot(wch[...], a2[c, k])
            t = jnp.tanh(l[0:ch] + bch)
            mix[c, k] = cot_q - cot_q * t * t
            raw_s[c, pl.ds(k, 1), :] = l[ch : ch + 1] * 2.0 + bd_ref[0]
            proj_s[c, pl.ds(k, 1), :] = 0.5 * (
                cot_sum + jnp.sum(cot * t, axis=0, keepdims=True)
            )
            return carry

        lax.fori_loop(0, slots, step, 0, unroll=unroll)

    def depth_of(c):
        span = pl.ds(c * rb, rb)
        raw = raw_s[c]
        live = (
            lax.broadcasted_iota(jnp.int32, raw.shape, 0) < live_ref[:, span]
        ).astype(F32)
        scale = gap_ref[:, span] * live
        soft = jnp.maximum(raw, 0.0) + jnp.log1p(jnp.exp(-jnp.abs(raw)))
        return raw, scale, soft * scale

    def summarize(c):
        raw, scale, depth = depth_of(c)
        total = jnp.zeros((1, rb), F32)
        for k in range(slots):
            ins_s[c, k : k + 1, :] = total
            total = total + depth[k : k + 1]
        weight = jnp.exp(-ins_s[c]) * (1.0 - jnp.exp(-depth))
        gath[c, me, 0:1, :] = total
        gath[c, me, 1:2, :] = jnp.sum(weight * proj_s[c], axis=0, keepdims=True)

    def copy_to(c, step):
        return pltpu.make_async_remote_copy(
            src_ref=gath.at[c, me],
            dst_ref=gath.at[c, me],
            send_sem=send_sem.at[c, step],
            recv_sem=recv_sem.at[c, step],
            device_id={"slab": lax.rem(me + step, slabs)},
            device_id_type=MESH,
        )

    def send(c):
        def go(step, carry):
            copy_to(c, step).start()
            return carry

        lax.fori_loop(1, slabs, go, 0)

    def receive(c):
        def go(step, carry):
            copy_to(c, step).wait()
            return carry

        lax.fori_loop(1, slabs, go, 0)

    def settle(c):
        span = pl.ds(c * rb, rb)
        raw, scale, depth = depth_of(c)
        zero = jnp.zeros((1, rb), F32)
        before, after, up, down = zero, zero, zero, zero
        for s in range(slabs):
            tau = gath[c, s, 0:1, :]
            light = gath[c, s, 1:2, :]
            before = before + jnp.where(s < me, tau, 0.0)
            after = after + jnp.where(s > me, tau, 0.0)
            down = jnp.where(s < me, light + jnp.exp(-tau) * down, down)
        for s in reversed(range(slabs)):
            tau = gath[c, s, 0:1, :]
            light = gath[c, s, 1:2, :]
            up = jnp.where(s > me, light + jnp.exp(-tau) * up, up)
        ascend = dir_ref[:, span] == 0
        prefix = jnp.where(ascend, before, after)
        behind = jnp.where(ascend, up, down)
        behind_out = jnp.exp(-(prefix + gath[c, me, 0:1, :])) * behind
        transmit = jnp.exp(-(prefix + ins_s[c]))
        fade = jnp.exp(-depth)
        weight = transmit * (1.0 - fade)
        sww[c] = weight
        sw_ref[:, span] = weight
        proj = proj_s[c]
        carried = weight * proj
        total = behind_out
        for k in reversed(range(slots)):
            beh_s[c, k : k + 1, :] = total
            total = total + carried[k : k + 1]
        dens = (transmit * fade * proj - beh_s[c]) * scale
        dens_ref[:, span] = dens
        rg_s[c] = dens * (0.5 * jnp.tanh(0.5 * raw) + 0.5)

    def backward(c):
        first_row = lax.broadcasted_iota(jnp.int32, (pad, rb), 0) == 0

        def color(k, carry):
            lg = mix[c, k] * sww[c, pl.ds(k, 1), :]
            tail = jnp.where(first_row, rg_s[c, pl.ds(k, 1), :], 0.0)
            lga = jnp.concatenate([lg.astype(BF16), tail.astype(BF16)], axis=0)
            d2_s[k] = (dot(wct[...], lga) * s2[c, k].astype(F32)).astype(BF16)
            gsum[:, hid : hid + ch + pad] += dot_nt(a2[c, k], lga)
            return carry

        def second(k, carry):
            d2 = d2_s[k]
            d1_s[k] = (dot(w2t[...], d2) * s1[c, k].astype(F32)).astype(BF16)
            gsum[:, 0:hid] += dot_nt(d2, a1[c, k])
            return carry

        def first(k, carry):
            d1 = d1_s[k]
            at_k = pl.ds(pl.multiple_of(k * feat, feat), feat)
            fp[c, at_k, :] = dot(w1t[...], d1).astype(BF16)
            gsum[:, hid + ch + pad : hid + ch + pad + feat] += dot_nt(d1, xp[c, at_k, :])
            return carry

        lax.fori_loop(0, slots, color, 0, unroll=unroll)
        lax.fori_loop(0, slots, second, 0, unroll=unroll)
        lax.fori_loop(0, slots, first, 0, unroll=unroll)

    for c in range(chunks):
        forward(c)
        summarize(c)
        if c == 0:
            pl.semaphore_wait(barrier, slabs)
        send(c)
    to = lax.broadcasted_iota(jnp.int32, permt.shape, 0)
    at = lax.broadcasted_iota(jnp.int32, permt.shape, 1)
    permt[...] = jnp.where(to == lax.rem(at, feat) * slots + at // feat, 1.0, 0.0).astype(BF16)
    gsum[...] = jnp.zeros_like(gsum)
    w1t[...] = w1_ref[...]
    w2t[...] = (w2_ref[...].astype(F32) * 0.5).T.astype(BF16)
    wct[...] = wch[...].astype(F32).T.astype(BF16)
    for c in range(chunks):
        receive(c)
        settle(c)
        backward(c)

    give = pltpu.make_async_remote_copy(
        src_ref=gsum.at[pl.ds(pl.multiple_of(other * half, half), half)],
        dst_ref=grecv,
        send_sem=wsem.at[0],
        recv_sem=wsem.at[1],
        device_id={"ray": other},
        device_id_type=MESH,
    )
    give.start()
    for c in range(chunks):
        feat_ref[:, pl.ds(c * rb, rb)] = dot(permt[...], fp[c]).astype(BF16)
    give.wait()
    both = gsum[pl.ds(pl.multiple_of(ray * half, half), half), :] + grecv[...]
    g2_ref[...] = both[:, 0:hid]
    turned = both[:, hid : hid + ch + pad].T
    gc_ref[...] = turned[0:ch]
    gs_ref[...] = turned[ch : ch + 1]
    g1_ref[...] = both[:, hid + ch + pad :].T[0:feat]


def write_kernel(
    feat_ref, dens_ref, sw_ref, g1_ref, g2_ref, gc_ref, gs_ref, cot_ref,
    feat_out, dens_out, rad_out, g1_out, g2_out, gc_out, gs_out,
    rad, sem, rad_sem,
):
    ch = cot_ref.shape[0]
    parts = rad_sem.shape[0]
    each = ch // parts
    pairs = (
        (feat_ref, feat_out), (g2_ref, g2_out), (gc_ref, gc_out), (g1_ref, g1_out),
        (dens_ref, dens_out), (gs_ref, gs_out),
    )
    copies = [pltpu.make_async_copy(src, dst, sem.at[i]) for i, (src, dst) in enumerate(pairs)]
    for copy in copies:
        copy.start()
    weight = sw_ref[...]
    for part in range(parts):
        for c in range(part * each, (part + 1) * each):
            rad[c] = (weight * cot_ref[c : c + 1, :]).astype(BF16)
        span = pl.ds(part * each, each)
        copy = pltpu.make_async_copy(rad.at[span], rad_out.at[span], rad_sem.at[part])
        copy.start()
        copies.append(copy)
    for copy in copies:
        copy.wait()


def body(
    slabs, features, spacing, live_counts, direction, cotangent, first_weight, first_bias,
    second_weight, second_bias, color_weight, color_bias, sigma_weight, sigma_bias,
):
    _, feat, slots, rays = features.shape
    hid = first_weight.shape[1]
    ch = color_weight.shape[1]
    padded = 128
    chunks = CHUNKS
    rb = rays // chunks
    half = hid // 2
    wide = hid + padded + 128
    rows = slots * feat
    vm = pl.BlockSpec(memory_space=pltpu.VMEM)
    hbm = pl.BlockSpec(memory_space=pltpu.HBM)
    S = jax.ShapeDtypeStruct
    V = pltpu.VMEM
    outs = pl.pallas_call(
        functools.partial(main_kernel, slabs, chunks, UNROLL),
        out_shape=(
            S((rows, rays), BF16), S((slots, rays), F32), S((slots, rays), F32),
            S((feat, half), F32), S((half, hid), F32), S((ch, half), F32), S((1, half), F32),
        ),
        in_specs=[pl.BlockSpec(memory_space=pltpu.SMEM)] + [hbm] * 12,
        out_specs=(vm,) * 7,
        scratch_shapes=[
            V((rows, rays), BF16), V((slots, rays), F32), V((1, rays), jnp.int32),
            V((1, rays), jnp.int32), V((ch, rays), F32), V((feat, hid), BF16), V((1, hid), F32),
            V((hid, hid), BF16), V((1, hid), F32), V((ch, hid), BF16), V((1, ch), F32),
            V((1, hid), BF16), pltpu.SemaphoreType.DMA((12,)),
            V((chunks, rows, rb), BF16), V((chunks, rows, rb), BF16), V((rows, rows), BF16), V((rows, rows), BF16),
            V((hid, feat), BF16), V((feat, hid), BF16), V((hid, hid), BF16), V((hid, hid), BF16),
            V((padded, hid), BF16), V((hid, padded), BF16),
            V((chunks, slots, hid, rb), BF16), V((chunks, slots, hid, rb), BF16),
            V((chunks, slots, hid, rb), BF16), V((chunks, slots, hid, rb), BF16),
            V((slots, hid, rb), BF16), V((slots, hid, rb), BF16),
            V((chunks, slots, ch, rb), F32),
            V((chunks, slots, rb), F32), V((chunks, slots, rb), F32), V((chunks, slots, rb), F32),
            V((chunks, slots, rb), F32), V((chunks, slots, rb), F32), V((chunks, slots, rb), F32),
            V((chunks, slabs, 2, rb), F32),
            V((hid, wide), F32), V((half, wide), F32),
            pltpu.SemaphoreType.DMA((chunks, slabs)),
            pltpu.SemaphoreType.DMA((chunks, slabs)),
            pltpu.SemaphoreType.DMA((2,)),
        ],
        compiler_params=pltpu.CompilerParams(
            collective_id=0, has_side_effects=True, vmem_limit_bytes=48 * 1024 * 1024
        ),
    )(
        sigma_bias,
        *(
            pltpu.with_memory_space_constraint(value, pltpu.HBM)
            for value in (
                features.reshape(rows, rays), spacing[0], live_counts, direction[None],
                cotangent, first_weight[0].T, first_bias, second_weight[0], second_bias,
                color_weight[0], color_bias, sigma_weight,
            )
        ),
    )
    feature_grad, dens, radiance_grad, g1, g2, gc, gs = pl.pallas_call(
        write_kernel,
        out_shape=(
            S((rows, rays), BF16), S((slots, rays), F32), S((ch, slots, rays), BF16),
            S((feat, half), F32), S((half, hid), F32), S((ch, half), F32), S((1, half), F32),
        ),
        in_specs=[vm] * 8,
        out_specs=(hbm,) * 7,
        scratch_shapes=[
            V((ch, slots, rays), BF16),
            pltpu.SemaphoreType.DMA((6,)),
            pltpu.SemaphoreType.DMA((4,)),
        ],
        compiler_params=pltpu.CompilerParams(vmem_limit_bytes=8 * 1024 * 1024),
    )(*outs, cotangent)
    return (
        feature_grad.reshape(1, feat, slots, rays), dens[None], radiance_grad[None],
        g1.T[None], g2[None], gc.T[None], gs,
    )


def solution(mesh):
    rays = P(("groups", "ray"))
    in_specs = (
        P("slab", None, None, ("groups", "ray")),
        P("slab", None, ("groups", "ray")),
        P("slab", ("groups", "ray")),
        rays,
        P(None, ("groups", "ray")),
        P("slab", None, None),
        P("slab", None),
        P("slab", None, None),
        P("slab", None),
        P("slab", None, None),
        P("slab", None),
        P("slab", None),
        P("slab"),
    )
    out_specs = (
        P("slab", None, None, ("groups", "ray")),
        P("slab", None, ("groups", "ray")),
        P("slab", None, None, ("groups", "ray")),
        P(("groups", "slab"), "ray", None),
        P(("groups", "slab"), "ray", None),
        P(("groups", "slab"), "ray", None),
        P(("groups", "slab"), "ray"),
    )
    return jax.shard_map(
        functools.partial(body, mesh.shape["slab"]),
        mesh=mesh,
        in_specs=in_specs,
        out_specs=out_specs,
        check_vma=False,
    )
```

```python
import functools

import jax
import jax.numpy as jnp
from jax import lax
from jax.experimental import pallas as pl
from jax.experimental.pallas import tpu as pltpu
from jax.sharding import PartitionSpec as P

MESH = pl.DeviceIdType.MESH
F32 = jnp.float32
BF16 = jnp.bfloat16
CHUNKS = 2
UNROLL = 8


def dot(a, b):
    return jnp.dot(a, b, preferred_element_type=F32)


def dot_nt(a, b):
    return lax.dot_general(a, b, (((1,), (1,)), ((), ())), preferred_element_type=F32)


def main_kernel(
    slabs, chunks, unroll,
    bd_ref, x_hbm, gap_hbm, live_hbm, dir_hbm, cot_hbm, w1_hbm, b1_hbm, w2_hbm, b2_hbm,
    wc_hbm, bc_hbm, wd_hbm,
    feat_ref, dens_ref, sw_ref, g1_ref, g2_ref, gc_ref, gs_ref,
    x_ref, gap_ref, live_ref, dir_ref, cot_ref, w1_ref, b1_ref, w2_ref, b2_ref,
    wc_ref, bc_ref, wd_ref, in_sem,
    xp, fp, perm, permt, w1h, w1t, w2h, w2t, wch, wct,
    a1, s1, a2, s2, d1_s, d2_s, mix, raw_s, proj_s, ins_s, beh_s, rg_s, sww,
    gath, gsum, grecv, send_sem, recv_sem, wsem,
):
    slots = gap_ref.shape[0]
    rays = gap_ref.shape[1]
    feat = w1_ref.shape[0]
    hid = w1_ref.shape[1]
    ch = wc_ref.shape[0]
    rb = rays // chunks
    half = hid // 2
    me = lax.axis_index("slab")
    ray = lax.axis_index("ray")
    other = 1 - ray

    barrier = pltpu.get_barrier_semaphore()

    def greet(step, carry):
        pl.semaphore_signal(
            barrier, inc=1, device_id={"slab": lax.rem(me + step, slabs)}, device_id_type=MESH
        )
        return carry

    lax.fori_loop(1, slabs, greet, 0, unroll=min(slabs - 1, 7))
    pl.semaphore_signal(barrier, inc=1, device_id={"ray": other}, device_id_type=MESH)

    loads = [
        pltpu.make_async_copy(src, dst, in_sem.at[i])
        for i, (src, dst) in enumerate(
            (
                (x_hbm, x_ref), (w1_hbm, w1_ref), (b1_hbm, b1_ref), (w2_hbm, w2_ref),
                (b2_hbm, b2_ref), (wc_hbm, wc_ref), (bc_hbm, bc_ref), (wd_hbm, wd_ref),
                (cot_hbm, cot_ref), (gap_hbm, gap_ref), (live_hbm, live_ref), (dir_hbm, dir_ref),
            )
        )
    ]
    for load in loads:
        load.start()

    first = lax.broadcasted_iota(jnp.int32, (feat, slots * feat), 0) * slots
    at = lax.broadcasted_iota(jnp.int32, (feat, slots * feat), 1)
    for k in range(slots):
        perm[k * feat : (k + 1) * feat, :] = jnp.where(at == first + k, 1.0, 0.0).astype(BF16)
    for load in loads[1:]:
        load.wait()

    w1h[...] = (w1_ref[...].astype(F32) * 0.5).T.astype(BF16)
    w2h[...] = w2_ref[...] * 0.5
    pad = wch.shape[0] - ch
    wrow = jnp.where(
        lax.broadcasted_iota(jnp.int32, (pad, hid), 0) == 0, wd_ref[...].astype(F32) * 0.5, 0.0
    )
    wch[0:ch, :] = wc_ref[...] * 0.5
    wch[ch:, :] = wrow.astype(BF16)

    def column(row):
        n = row.shape[1]
        return jnp.broadcast_to(row * 0.5, (8, n)).T[:, 0:1]

    b1h = column(b1_ref[...])
    b2h = column(b2_ref[...])
    bch = column(bc_ref[...])
    loads[0].wait()

    def forward(c):
        span = pl.ds(c * rb, rb)
        xp[c] = dot(perm[...], x_ref[:, span]).astype(BF16)
        cot = cot_ref[:, span]
        cot_q = cot * 0.25
        cot_sum = jnp.sum(cot, axis=0, keepdims=True)

        def first(k, carry):
            xk = xp[c, pl.ds(pl.multiple_of(k * feat, feat), feat), :]
            u = dot(w1h[...], xk) + b1h
            t = jnp.tanh(u)
            p = 1.0 + t
            a = u * p
            a1[c, k] = a.astype(BF16)
            s1[c, k] = (p + a * (1.0 - t)).astype(BF16)
            return carry

        def second(k, carry):
            u = dot(w2h[...], a1[c, k]) + b2h
            t = jnp.tanh(u)
            p = 1.0 + t
            a = u * p
            a2[c, k] = a.astype(BF16)
            s2[c, k] = (p + a * (1.0 - t)).astype(BF16)
            return carry

        def color(k, carry):
            l = dot(wch[...], a2[c, k])
            t = jnp.tanh(l[0:ch] + bch)
            mix[c, k] = cot_q - cot_q * t * t
            raw_s[c, pl.ds(k, 1), :] = l[ch : ch + 1] * 2.0 + bd_ref[0]
            proj_s[c, pl.ds(k, 1), :] = 0.5 * (
                cot_sum + jnp.sum(cot * t, axis=0, keepdims=True)
            )
            return carry

        lax.fori_loop(0, slots, first, 0, unroll=unroll)
        lax.fori_loop(0, slots, second, 0, unroll=unroll)
        lax.fori_loop(0, slots, color, 0, unroll=unroll)

    def depth_of(c):
        span = pl.ds(c * rb, rb)
        raw = raw_s[c]
        live = (
            lax.broadcasted_iota(jnp.int32, raw.shape, 0) < live_ref[:, span]
        ).astype(F32)
        scale = gap_ref[:, span] * live
        soft = jnp.maximum(raw, 0.0) + jnp.log1p(jnp.exp(-jnp.abs(raw)))
        return raw, scale, soft * scale

    def summarize(c):
        raw, scale, depth = depth_of(c)
        total = jnp.zeros((1, rb), F32)
        for k in range(slots):
            ins_s[c, k : k + 1, :] = total
            total = total + depth[k : k + 1]
        weight = jnp.exp(-ins_s[c]) * (1.0 - jnp.exp(-depth))
        gath[c, me, 0:1, :] = total
        gath[c, me, 1:2, :] = jnp.sum(weight * proj_s[c], axis=0, keepdims=True)

    def copy_to(c, step):
        return pltpu.make_async_remote_copy(
            src_ref=gath.at[c, me],
            dst_ref=gath.at[c, me],
            send_sem=send_sem.at[c, step],
            recv_sem=recv_sem.at[c, step],
            device_id={"slab": lax.rem(me + step, slabs)},
            device_id_type=MESH,
        )

    def send(c):
        def go(step, carry):
            copy_to(c, step).start()
            return carry

        lax.fori_loop(1, slabs, go, 0, unroll=min(slabs - 1, 7))

    def receive(c):
        def go(step, carry):
            copy_to(c, step).wait()
            return carry

        lax.fori_loop(1, slabs, go, 0, unroll=min(slabs - 1, 7))

    def settle(c):
        span = pl.ds(c * rb, rb)
        raw, scale, depth = depth_of(c)
        zero = jnp.zeros((1, rb), F32)
        before, after, up, down = zero, zero, zero, zero
        for s in range(slabs):
            tau = gath[c, s, 0:1, :]
            light = gath[c, s, 1:2, :]
            before = before + jnp.where(s < me, tau, 0.0)
            after = after + jnp.where(s > me, tau, 0.0)
            down = jnp.where(s < me, light + jnp.exp(-tau) * down, down)
        for s in reversed(range(slabs)):
            tau = gath[c, s, 0:1, :]
            light = gath[c, s, 1:2, :]
            up = jnp.where(s > me, light + jnp.exp(-tau) * up, up)
        ascend = dir_ref[:, span] == 0
        prefix = jnp.where(ascend, before, after)
        behind = jnp.where(ascend, up, down)
        behind_out = jnp.exp(-(prefix + gath[c, me, 0:1, :])) * behind
        transmit = jnp.exp(-(prefix + ins_s[c]))
        fade = jnp.exp(-depth)
        weight = transmit * (1.0 - fade)
        sww[c] = weight
        sw_ref[:, span] = weight
        proj = proj_s[c]
        carried = weight * proj
        total = behind_out
        for k in reversed(range(slots)):
            beh_s[c, k : k + 1, :] = total
            total = total + carried[k : k + 1]
        dens = (transmit * fade * proj - beh_s[c]) * scale
        dens_ref[:, span] = dens
        rg_s[c] = dens * (0.5 * jnp.tanh(0.5 * raw) + 0.5)

    def backward(c):
        first_row = lax.broadcasted_iota(jnp.int32, (pad, rb), 0) == 0

        def color(k, carry):
            lg = mix[c, k] * sww[c, pl.ds(k, 1), :]
            tail = jnp.where(first_row, rg_s[c, pl.ds(k, 1), :], 0.0)
            lga = jnp.concatenate([lg.astype(BF16), tail.astype(BF16)], axis=0)
            d2_s[k] = (dot(wct[...], lga) * s2[c, k].astype(F32)).astype(BF16)
            gsum[:, hid : hid + ch + pad] += dot_nt(a2[c, k], lga)
            return carry

        def second(k, carry):
            d2 = d2_s[k]
            d1_s[k] = (dot(w2t[...], d2) * s1[c, k].astype(F32)).astype(BF16)
            gsum[:, 0:hid] += dot_nt(d2, a1[c, k])
            return carry

        def first(k, carry):
            d1 = d1_s[k]
            at_k = pl.ds(pl.multiple_of(k * feat, feat), feat)
            fp[c, at_k, :] = dot(w1t[...], d1).astype(BF16)
            gsum[:, hid + ch + pad : hid + ch + pad + feat] += dot_nt(d1, xp[c, at_k, :])
            return carry

        lax.fori_loop(0, slots, color, 0, unroll=unroll)
        lax.fori_loop(0, slots, second, 0, unroll=unroll)
        lax.fori_loop(0, slots, first, 0, unroll=unroll)

    for c in range(chunks):
        forward(c)
        summarize(c)
        if c == 0:
            pl.semaphore_wait(barrier, slabs)
        send(c)
    to = lax.broadcasted_iota(jnp.int32, permt.shape, 0)
    at = lax.broadcasted_iota(jnp.int32, permt.shape, 1)
    permt[...] = jnp.where(to == lax.rem(at, feat) * slots + at // feat, 1.0, 0.0).astype(BF16)
    gsum[...] = jnp.zeros_like(gsum)
    w1t[...] = w1_ref[...]
    w2t[...] = (w2_ref[...].astype(F32) * 0.5).T.astype(BF16)
    wct[...] = wch[...].astype(F32).T.astype(BF16)
    for c in range(chunks):
        receive(c)
        settle(c)
        backward(c)

    give = pltpu.make_async_remote_copy(
        src_ref=gsum.at[pl.ds(pl.multiple_of(other * half, half), half)],
        dst_ref=grecv,
        send_sem=wsem.at[0],
        recv_sem=wsem.at[1],
        device_id={"ray": other},
        device_id_type=MESH,
    )
    give.start()
    for c in range(chunks):
        feat_ref[:, pl.ds(c * rb, rb)] = dot(permt[...], fp[c]).astype(BF16)
    give.wait()
    both = gsum[pl.ds(pl.multiple_of(ray * half, half), half), :] + grecv[...]
    g2_ref[...] = both[:, 0:hid]
    turned = both[:, hid : hid + ch + pad].T
    gc_ref[...] = turned[0:ch]
    gs_ref[...] = turned[ch : ch + 1]
    g1_ref[...] = both[:, hid + ch + pad :].T[0:feat]


def write_kernel(
    feat_ref, dens_ref, sw_ref, g1_ref, g2_ref, gc_ref, gs_ref, cot_ref,
    feat_out, dens_out, rad_out, g1_out, g2_out, gc_out, gs_out,
    rad, sem, rad_sem,
):
    ch = cot_ref.shape[0]
    parts = rad_sem.shape[0]
    each = ch // parts
    pairs = (
        (feat_ref, feat_out), (g2_ref, g2_out), (gc_ref, gc_out), (g1_ref, g1_out),
        (dens_ref, dens_out), (gs_ref, gs_out),
    )
    copies = [pltpu.make_async_copy(src, dst, sem.at[i]) for i, (src, dst) in enumerate(pairs)]
    for copy in copies:
        copy.start()
    weight = sw_ref[...]
    for part in range(parts):
        for c in range(part * each, (part + 1) * each):
            rad[c] = (weight * cot_ref[c : c + 1, :]).astype(BF16)
        span = pl.ds(part * each, each)
        copy = pltpu.make_async_copy(rad.at[span], rad_out.at[span], rad_sem.at[part])
        copy.start()
        copies.append(copy)
    for copy in copies:
        copy.wait()


def body(
    slabs, features, spacing, live_counts, direction, cotangent, first_weight, first_bias,
    second_weight, second_bias, color_weight, color_bias, sigma_weight, sigma_bias,
):
    _, feat, slots, rays = features.shape
    hid = first_weight.shape[1]
    ch = color_weight.shape[1]
    padded = 128
    chunks = CHUNKS
    rb = rays // chunks
    half = hid // 2
    wide = hid + padded + 128
    rows = slots * feat
    vm = pl.BlockSpec(memory_space=pltpu.VMEM)
    hbm = pl.BlockSpec(memory_space=pltpu.HBM)
    S = jax.ShapeDtypeStruct
    V = pltpu.VMEM
    outs = pl.pallas_call(
        functools.partial(main_kernel, slabs, chunks, UNROLL),
        out_shape=(
            S((rows, rays), BF16), S((slots, rays), F32), S((slots, rays), F32),
            S((feat, half), F32), S((half, hid), F32), S((ch, half), F32), S((1, half), F32),
        ),
        in_specs=[pl.BlockSpec(memory_space=pltpu.SMEM)] + [hbm] * 12,
        out_specs=(vm,) * 7,
        scratch_shapes=[
            V((rows, rays), BF16), V((slots, rays), F32), V((1, rays), jnp.int32),
            V((1, rays), jnp.int32), V((ch, rays), F32), V((feat, hid), BF16), V((1, hid), F32),
            V((hid, hid), BF16), V((1, hid), F32), V((ch, hid), BF16), V((1, ch), F32),
            V((1, hid), BF16), pltpu.SemaphoreType.DMA((12,)),
            V((chunks, rows, rb), BF16), V((chunks, rows, rb), BF16), V((rows, rows), BF16), V((rows, rows), BF16),
            V((hid, feat), BF16), V((feat, hid), BF16), V((hid, hid), BF16), V((hid, hid), BF16),
            V((padded, hid), BF16), V((hid, padded), BF16),
            V((chunks, slots, hid, rb), BF16), V((chunks, slots, hid, rb), BF16),
            V((chunks, slots, hid, rb), BF16), V((chunks, slots, hid, rb), BF16),
            V((slots, hid, rb), BF16), V((slots, hid, rb), BF16),
            V((chunks, slots, ch, rb), F32),
            V((chunks, slots, rb), F32), V((chunks, slots, rb), F32), V((chunks, slots, rb), F32),
            V((chunks, slots, rb), F32), V((chunks, slots, rb), F32), V((chunks, slots, rb), F32),
            V((chunks, slabs, 2, rb), F32),
            V((hid, wide), F32), V((half, wide), F32),
            pltpu.SemaphoreType.DMA((chunks, slabs)),
            pltpu.SemaphoreType.DMA((chunks, slabs)),
            pltpu.SemaphoreType.DMA((2,)),
        ],
        compiler_params=pltpu.CompilerParams(
            collective_id=0, has_side_effects=True, vmem_limit_bytes=48 * 1024 * 1024
        ),
    )(
        sigma_bias,
        *(
            pltpu.with_memory_space_constraint(value, pltpu.HBM)
            for value in (
                features.reshape(rows, rays), spacing[0], live_counts, direction[None],
                cotangent, first_weight[0].T, first_bias, second_weight[0], second_bias,
                color_weight[0], color_bias, sigma_weight,
            )
        ),
    )
    feature_grad, dens, radiance_grad, g1, g2, gc, gs = pl.pallas_call(
        write_kernel,
        out_shape=(
            S((rows, rays), BF16), S((slots, rays), F32), S((ch, slots, rays), BF16),
            S((feat, half), F32), S((half, hid), F32), S((ch, half), F32), S((1, half), F32),
        ),
        in_specs=[vm] * 8,
        out_specs=(hbm,) * 7,
        scratch_shapes=[
            V((ch, slots, rays), BF16),
            pltpu.SemaphoreType.DMA((6,)),
            pltpu.SemaphoreType.DMA((4,)),
        ],
        compiler_params=pltpu.CompilerParams(vmem_limit_bytes=8 * 1024 * 1024),
    )(*outs, cotangent)
    return (
        feature_grad.reshape(1, feat, slots, rays), dens[None], radiance_grad[None],
        g1.T[None], g2[None], gc.T[None], gs,
    )


def solution(mesh):
    rays = P(("groups", "ray"))
    in_specs = (
        P("slab", None, None, ("groups", "ray")),
        P("slab", None, ("groups", "ray")),
        P("slab", ("groups", "ray")),
        rays,
        P(None, ("groups", "ray")),
        P("slab", None, None),
        P("slab", None),
        P("slab", None, None),
        P("slab", None),
        P("slab", None, None),
        P("slab", None),
        P("slab", None),
        P("slab"),
    )
    out_specs = (
        P("slab", None, None, ("groups", "ray")),
        P("slab", None, ("groups", "ray")),
        P("slab", None, None, ("groups", "ray")),
        P(("groups", "slab"), "ray", None),
        P(("groups", "slab"), "ray", None),
        P(("groups", "slab"), "ray", None),
        P(("groups", "slab"), "ray"),
    )
    return jax.shard_map(
        functools.partial(body, mesh.shape["slab"]),
        mesh=mesh,
        in_specs=in_specs,
        out_specs=out_specs,
        check_vma=False,
    )
```
